32 devices in a mesh: ctx: 4 (over y, core), ep: 8 (over z, x).
Axes of the slice: x: 2, y: 2, z: 4, core: 2. Of those that a mesh axis runs over, the one named last changes fastest.
Arguments:
- queries: bfloat16 [1024, 1, 2048], P('ctx', None, 'ep'), may hold values from -6 to 6
- keys_in: bfloat16 [1024, 1, 2048], P('ctx', None, 'ep'), may hold values from -6 to 6
- values_in: bfloat16 [1024, 1, 2048], P('ctx', None, 'ep'), may hold values from -6 to 6
- log_decay: float32 [16, 1, 1024], P('ep', None, 'ctx'), may hold values from -1.5 to 0
- attn_gain: float32 [2048], P('ep'), may hold values from 0.1 to 1.9
- out_weight: bfloat16 [2048, 6144], P('ep', 'ctx'), may hold values from -0.125 to 0.125
- residual: bfloat16 [1024, 1, 6144], P(('ctx', 'ep')), may hold values from -42 to 42
- moe_gain: float32 [6144], replicated, may hold values from 0.1 to 1.9
- router: bfloat16 [6144, 8], replicated, may hold values from -0.078125 to 0.078125
- gate_weight: bfloat16 [8, 6144, 4608], P('ep', None, 'ctx'), may hold values from -0.078125 to 0.078125
- up_weight: bfloat16 [8, 6144, 4608], P('ep', None, 'ctx'), may hold values from -0.078125 to 0.078125
- down_weight: bfloat16 [8, 4608, 6144], P('ep', 'ctx'), may hold values from -0.09375 to 0.09375
- routes: int32 [1024, 1, 2], P(('ctx', 'ep')), may hold values from 0 to 7, all different within a row; in each aligned block of 32 rows (0 to 31, 32 to 63, ..., all dimensions but the last counted through in order) at most 12 rows name the same one
Outputs:
- mixed: bfloat16 [1024, 1, 6144], P(('ctx', 'ep'))
The draws below stay inside these ranges and needn't reach their ends.
Inputs may be any that keep to these rules, and one draw needn't show every extreme that they name: `routes`: each row names two different experts. Among the tokens of one device (aligned blocks of 32 rows of the flattened positions and sequences) no expert is named more than 12 times.
All inputs are finite; a program needn't handle non-finite values.
Results may differ from the reference program's by a relative error of at most 0.017.
Values may be sent and summed in bfloat16 or wider, within the bound.
No kernel may reach another device: no remote copies, remote signals or barrier semaphores. Data moves between devices by JAX's collectives and lax.ppermute only.
A program may use at most 128 MiB of HBM per device.

```python
import math
import jax
import jax.numpy as jnp
import numpy as np
from jax import lax

D = 6144
HD = 128
HEADS_DEV = 2
FF = 4608
SPAN = 256
SEQUENCE_COUNT = 1
HEAD_TOTAL = 16
EXPERTS = 8
SEQUENCE_LENGTH = 1024
ROWS = 32
CAP = 12
N_CTX = 4
N_EP = 8


def draw_log_decay(key, part):
    sequence_streams = jax.random.split(key, 7)
    fast_share = 0.5
    quick = jax.random.bernoulli(sequence_streams[0], fast_share, (HEAD_TOTAL, 1, 1))
    fast_rate = jnp.exp(jax.random.uniform(sequence_streams[1], (HEAD_TOTAL, 1, 1), jnp.float32, jnp.log(1.0 / 50.0), jnp.log(1.0 / 30.0)))
    slow_rate = jax.random.uniform(sequence_streams[2], (HEAD_TOTAL, 1, 1), jnp.float32, 0.05, 0.2) / SEQUENCE_LENGTH
    baseline_rate = jnp.where(quick, fast_rate, slow_rate)
    blocks = SEQUENCE_LENGTH // SPAN
    block_multiplier = jnp.exp(jax.random.uniform(sequence_streams[3], (HEAD_TOTAL, SEQUENCE_COUNT, blocks, 1), jnp.float32, jnp.log(0.5), jnp.log(2.0)))
    block_multiplier = jnp.broadcast_to(block_multiplier, (HEAD_TOTAL, SEQUENCE_COUNT, blocks, SPAN)).reshape(HEAD_TOTAL, SEQUENCE_COUNT, SEQUENCE_LENGTH)
    jitter_level = jax.random.uniform(sequence_streams[4], (HEAD_TOTAL, SEQUENCE_COUNT, SEQUENCE_LENGTH), jnp.float32, 0.5, 1.5)
    spike_position = jax.random.randint(sequence_streams[5], (HEAD_TOTAL, SEQUENCE_COUNT, 2, 1), 0, SEQUENCE_LENGTH)
    token_position = jnp.arange(SEQUENCE_LENGTH, dtype=jnp.int32)[None, None, None, :]
    spike_events = jnp.sum((token_position == spike_position).astype(jnp.float32), axis=2)
    spike_depth = jax.random.uniform(sequence_streams[6], (HEAD_TOTAL, SEQUENCE_COUNT, SEQUENCE_LENGTH), jnp.float32, 0.22, 0.69)
    return -(baseline_rate * block_multiplier * jitter_level) - spike_events * spike_depth


def draw_residual(key, part):
    sequence_streams = jax.random.split(key, 1)
    drawn = jnp.clip(jax.random.normal(sequence_streams[0], (SEQUENCE_LENGTH, SEQUENCE_COUNT, D), jnp.float32), -6.0, 6.0)
    return drawn.astype(jnp.bfloat16)


def level_of(own_key, dims, shards, low, largest):
    def one(position, parts):
        steps = jax.random.uniform(jax.random.fold_in(jax.random.fold_in(own_key, 6), position), (parts,), jnp.float32, low / len(shards), largest / len(shards))
        return jnp.repeat(jnp.exp(steps), dims[position] // parts).reshape((-1,) + (1,) * (len(dims) - position - 1))

    level = one(*shards[0])
    for cut in shards[1:]:
        level = level * one(*cut)
    return level


def assign_block(own_key, own, number, rows, number_of, top, limit, skew):
    sequence = jax.random.permutation(own_key, number_of)
    heavy_load, common = shares(number_of, rows * top, limit, skew, True), shares(number_of, rows * top, limit, skew, False)
    places = jnp.arange(number_of)

    def named(lengths, turn):
        used = int((lengths > 0).sum())
        fixed = max(1, used // 4)
        moved = fixed + (places - fixed + turn * (used - fixed)) % max(1, number_of - fixed)
        return jnp.zeros((number_of,), jnp.int32).at[sequence[jnp.where(places < fixed, places, moved)]].set(jnp.asarray(lengths, jnp.int32))

    lengths = jnp.where(number % 4 == 0, named(heavy_load, number // 4), named(common, number - number // 4 - 1))
    mixed = jax.random.permutation(jax.random.fold_in(own, 3), number_of)
    donor, sink = mixed[0:number_of // 2 * 2:2], mixed[1:number_of // 2 * 2:2]
    margin = jnp.minimum(lengths[donor] - 1, limit - lengths[sink]) // 2
    margin = jnp.where((donor == sequence[0]) | (sink == sequence[0]) | (lengths[sink] == 0), 0, jnp.maximum(margin, 0))
    moved = jax.random.randint(jax.random.fold_in(own, 4), (number_of // 2,), 0, 1 << 20) % (margin + 1)
    lengths = lengths.at[donor].add(-moved).at[sink].add(moved)
    items = jnp.searchsorted(jnp.cumsum(lengths), jnp.arange(rows * top), side="right").astype(jnp.int32)
    table = items.reshape(top, rows).T
    table = table[jax.random.permutation(jax.random.fold_in(own, 1), rows)]
    turn = jax.random.randint(jax.random.fold_in(own, 2), (rows, 1), 0, top)
    return jnp.take_along_axis(table, (jnp.arange(top)[None, :] + turn) % top, axis=1)


def shares(count, total, most, lean, full):
    weights = [(1 << 20) // math.isqrt(standing ** lean) + 1 for standing in range(1, count + 1)]
    largest = most if full else min(most, max(-(-total // count), total * weights[0] // sum(weights)))
    least = 1 if total - largest >= count - 1 else 0
    counts, surplus = [largest] + [least] * (count - 1), total - largest - least * (count - 1)
    while surplus > 0:
        free = [i for i in range(1, count) if counts[i] < largest] or [i for i in range(1, count) if counts[i] < most]
        pool, left = sum([weights[i] for i in free]), surplus
        for i in free:
            addition = min(most - counts[i], max(1, left * weights[i] // pool), surplus)
            counts[i] = counts[i] + addition
            surplus = surplus - addition
    return np.array(counts)


def scatter_about(key, extent, scale, bound, cuts=(), kind=jnp.bfloat16):
    factor_of = level_of(key, extent, cuts, -0.22, 0.18) if cuts else 1.0
    values = jax.random.normal(key, extent, jnp.float32) * scale * factor_of
    return jnp.minimum(jnp.maximum(values, -bound), bound).astype(kind)


def setup_inputs(seed: int = 0) -> dict:
    keys = jax.random.split(jax.random.key(seed), 14)
    queries = scatter_about(keys[0], (SEQUENCE_LENGTH, SEQUENCE_COUNT, HEAD_TOTAL * HD), 1.0, 6.0, ((0, 4), (2, 8)))
    keys_in = scatter_about(keys[1], (SEQUENCE_LENGTH, SEQUENCE_COUNT, HEAD_TOTAL * HD), 1.0, 6.0, ((0, 4), (2, 8)))
    values_in = scatter_about(keys[2], (SEQUENCE_LENGTH, SEQUENCE_COUNT, HEAD_TOTAL * HD), 1.0, 6.0, ((0, 4), (2, 8)))
    log_decay = draw_log_decay(jax.random.fold_in(keys[13], 71), 0)
    attn_gain = jnp.clip(1.0 + 0.18 * jax.random.normal(keys[4], (HEAD_TOTAL * HD,), jnp.float32), 0.1, 1.9)
    out_weight = scatter_about(keys[5], (HEAD_TOTAL * HD, D), (HEAD_TOTAL * HD) ** -0.5, 0.125, ((0, 8), (1, 4)))
    residual = draw_residual(jax.random.fold_in(keys[13], 71), 0)
    moe_gain = jnp.clip(1.0 + 0.18 * jax.random.normal(keys[7], (D,), jnp.float32), 0.1, 1.9)
    router = scatter_about(keys[8], (D, EXPERTS), D ** -0.5, 0.078125)
    gate_weight = scatter_about(keys[9], (EXPERTS, D, FF), D ** -0.5, 0.078125, ((0, 8), (2, 4)))
    up_weight = scatter_about(keys[10], (EXPERTS, D, FF), D ** -0.5, 0.078125, ((0, 8), (2, 4)))
    down_weight = scatter_about(keys[11], (EXPERTS, FF, D), FF ** -0.5, 0.09375, ((0, 8), (1, 4)))
    routes_keys = jax.random.split(jax.random.fold_in(keys[12], 1), SEQUENCE_LENGTH * SEQUENCE_COUNT // ROWS)
    routes_turns = jax.random.permutation(jax.random.fold_in(keys[12], 3), SEQUENCE_LENGTH * SEQUENCE_COUNT // ROWS)
    routes = jax.vmap(lambda own, number: assign_block(jax.random.fold_in(keys[12], 2), own, number, ROWS, EXPERTS, 2, CAP, 1))(routes_keys, routes_turns).reshape((SEQUENCE_LENGTH, SEQUENCE_COUNT, 2))
    return {"queries": queries, "keys_in": keys_in, "values_in": values_in, "log_decay": log_decay, "attn_gain": attn_gain, "out_weight": out_weight, "residual": residual, "moe_gain": moe_gain, "router": router, "gate_weight": gate_weight, "up_weight": up_weight, "down_weight": down_weight, "routes": routes}


highest = lax.Precision.HIGHEST

def silu_float(values):
    return values * jax.nn.sigmoid(values)

def lightning(queries, keys_in, values_in, log_decay):
    blocks = SEQUENCE_LENGTH // SPAN
    q_all = silu_float(queries.astype(jnp.float32)).reshape(blocks, SPAN, SEQUENCE_COUNT, HEAD_TOTAL, HD)
    k_all = silu_float(keys_in.astype(jnp.float32)).reshape(blocks, SPAN, SEQUENCE_COUNT, HEAD_TOTAL, HD)
    v_all = values_in.astype(jnp.float32).reshape(blocks, SPAN, SEQUENCE_COUNT, HEAD_TOTAL, HD)
    decay_blocks = jnp.transpose(log_decay.reshape(HEAD_TOTAL, SEQUENCE_COUNT, blocks, SPAN), (2, 1, 0, 3))
    positions = jnp.arange(SPAN, dtype=jnp.int32)
    causal = positions[:, None] >= positions[None, :]

    def advance(state, pieces):
        q_block, k_block, v_block, decay_block = pieces
        cumulative = jnp.cumsum(decay_block, axis=-1)
        spacing = cumulative[..., :, None] - cumulative[..., None, :]
        damping = jnp.where(causal, jnp.exp(jnp.where(causal, spacing, 0.0)), 0.0)
        scores = jnp.einsum('tshd,ushd->shtu', q_block, k_block, precision=highest) * damping
        inside = jnp.einsum('shtu,ushe->tshe', scores, v_block, precision=highest)
        carried = jnp.exp(jnp.transpose(cumulative, (2, 0, 1)))[..., None] * jnp.einsum('tshd,shde->tshe', q_block, state, precision=highest)
        remaining = jnp.exp(cumulative[..., -1:] - cumulative)
        fresh_state = jnp.einsum('ushd,ushe->shde', k_block * jnp.transpose(remaining, (2, 0, 1))[..., None], v_block, precision=highest)
        new_state = jnp.exp(cumulative[..., -1])[..., None, None] * state + fresh_state
        return (new_state, inside + carried)
    start_state = jnp.zeros((SEQUENCE_COUNT, HEAD_TOTAL, HD, HD), jnp.float32)
    _, outputs = lax.scan(advance, start_state, (q_all, k_all, v_all, decay_blocks))
    return outputs.reshape(SEQUENCE_LENGTH, SEQUENCE_COUNT, HEAD_TOTAL, HD)

def reference(queries, keys_in, values_in, log_decay, attn_gain, out_weight, residual, moe_gain, router, gate_weight, up_weight, down_weight, routes):
    tokens = SEQUENCE_LENGTH * SEQUENCE_COUNT
    heads_out = lightning(queries, keys_in, values_in, log_decay)
    mean_square = lax.optimization_barrier(jnp.mean(heads_out * heads_out, axis=-1, keepdims=True))
    normed_heads = (heads_out * lax.rsqrt(mean_square + 1e-06) * attn_gain.reshape(HEAD_TOTAL, HD)).astype(jnp.bfloat16)
    grouped = jnp.transpose(normed_heads.reshape(tokens, N_EP, HEADS_DEV * HD), (1, 0, 2))
    grouped_weight = out_weight.reshape(N_EP, HEADS_DEV * HD, D)

    def add_group(running, pieces):
        group_in, group_weight = pieces
        partial_value = jnp.dot(group_in, group_weight, preferred_element_type=jnp.float32).astype(jnp.bfloat16)
        partial_value = lax.optimization_barrier(partial_value).astype(jnp.float32)
        return (running + partial_value, None)
    attn, _ = lax.scan(add_group, jnp.zeros((tokens, D), jnp.float32), (grouped, grouped_weight))
    hidden_state = residual.reshape(tokens, D).astype(jnp.float32) + attn
    moe_scale = lax.rsqrt(lax.optimization_barrier(jnp.mean(hidden_state * hidden_state, axis=-1, keepdims=True)) + 1e-06)
    moe_in = (hidden_state * moe_scale * moe_gain).astype(jnp.bfloat16)
    logits = jnp.dot(moe_in, router, preferred_element_type=jnp.float32)
    expert_ids = routes.reshape(tokens, 2).astype(jnp.int32)
    picked = jnp.take_along_axis(logits, expert_ids, axis=1)
    weight_first = jax.nn.sigmoid(picked[:, 0] - picked[:, 1])
    weight_second = jax.nn.sigmoid(picked[:, 1] - picked[:, 0])
    blocks = tokens // ROWS
    block_ids = expert_ids.reshape(blocks, 2 * ROWS)
    route_hot = (block_ids[..., None] == jnp.arange(EXPERTS, dtype=jnp.int32)).astype(jnp.int32)
    earlier = jnp.cumsum(route_hot, axis=1) - route_hot
    slots = lax.optimization_barrier(jnp.sum(earlier * route_hot, axis=-1)).astype(jnp.int32)
    owner_row = jnp.repeat(jnp.arange(tokens, dtype=jnp.int32).reshape(blocks, ROWS), 2, axis=1)
    block_index = jnp.broadcast_to(jnp.arange(blocks, dtype=jnp.int32)[:, None], (blocks, 2 * ROWS))
    table = jnp.full((EXPERTS, blocks, CAP), tokens, jnp.int32)
    table = table.at[block_ids, block_index, slots].set(owner_row)
    padded_in = jnp.concatenate([moe_in, jnp.zeros((1, D), jnp.bfloat16)], axis=0)
    expert_inputs = padded_in[table.reshape(EXPERTS, blocks * CAP)]

    def one_expert(pieces):
        rows_in, gate_part, up_part, down_part = pieces
        gate_out = jnp.dot(rows_in, gate_part, preferred_element_type=jnp.float32)
        up_out = jnp.dot(rows_in, up_part, preferred_element_type=jnp.float32)
        expert_hidden = (silu_float(gate_out) * up_out).astype(jnp.bfloat16)
        hidden_groups = jnp.transpose(expert_hidden.reshape(blocks * CAP, N_CTX, FF // N_CTX), (1, 0, 2))
        down_groups = down_part.reshape(N_CTX, FF // N_CTX, D)

        def add_slice(running, sliced):
            slice_hidden, slice_down = sliced
            partial_value = jnp.dot(slice_hidden, slice_down, preferred_element_type=jnp.float32).astype(jnp.bfloat16)
            partial_value = lax.optimization_barrier(partial_value).astype(jnp.float32)
            return (running + partial_value, None)
        summed, _ = lax.scan(add_slice, jnp.zeros((blocks * CAP, D), jnp.float32), (hidden_groups, down_groups))
        return summed.astype(jnp.bfloat16)
    expert_out = lax.map(one_expert, (expert_inputs, gate_weight, up_weight, down_weight))
    flat_index = block_ids * (blocks * CAP) + block_index * CAP + slots
    fetched = expert_out.reshape(EXPERTS * blocks * CAP, D)[flat_index.reshape(tokens, 2)].astype(jnp.float32)
    mixed = hidden_state + weight_first[:, None] * fetched[:, 0] + weight_second[:, None] * fetched[:, 1]
    return mixed.astype(jnp.bfloat16).reshape(SEQUENCE_LENGTH, SEQUENCE_COUNT, D)
```

```python
import jax
import jax.numpy as jnp
from jax import lax
from jax.sharding import PartitionSpec as P

highest = lax.Precision.HIGHEST
f32, bf16 = jnp.float32, jnp.bfloat16


def entering(array, axis, join, neutral):
    place = lax.axis_index(axis)
    gathered = jax.tree.map(
        lambda a, kind: lax.all_gather(a.astype(kind), axis), array, (bf16, bf16)
    )
    state = jax.tree.map(lambda a, e: jnp.zeros_like(a) + jnp.asarray(e, a.dtype), array, neutral)

    def one(hop, state):
        return join(
            state,
            jax.tree.map(
                lambda a, own: lax.dynamic_index_in_dim(a, hop, 0, False).astype(own.dtype),
                gathered,
                array,
            ),
        )

    return lax.fori_loop(0, place, one, state)


def silu_float(values):
    return values * jax.nn.sigmoid(values)


def swap(array, axis, mask):
    size = lax.axis_size(axis)
    return lax.ppermute(array, axis, [(i, i ^ mask) for i in range(size)])


def absolute(items, me):
    items, bit = list(items), 1
    while bit < len(items):
        flip = (me & bit) != 0
        items = [jnp.where(flip, items[i ^ bit], items[i]) for i in range(len(items))]
        bit *= 2
    return items


def attention(queries, keys_in, values_in, log_decay, attn_gain):
    length, sequences, width = queries.shape
    head_count = log_decay.shape[0]
    head_size = width // head_count
    split = (length, sequences, head_count, head_size)
    q_local = silu_float(queries.astype(f32)).reshape(split)
    k_local = silu_float(keys_in.astype(f32)).reshape(split)
    v_local = values_in.astype(f32).reshape(split)
    cumulative = jnp.cumsum(jnp.transpose(log_decay, (1, 0, 2)), axis=-1)
    positions = jnp.arange(length, dtype=jnp.int32)
    causal = positions[:, None] >= positions[None, :]
    spacing = cumulative[..., :, None] - cumulative[..., None, :]
    damping = jnp.where(causal, jnp.exp(jnp.where(causal, spacing, 0.0)), 0.0)
    scores = jnp.einsum("tshd,ushd->shtu", q_local, k_local, precision=highest) * damping
    inside = jnp.einsum("shtu,ushe->tshe", scores, v_local, precision=highest)
    remaining = jnp.exp(cumulative[..., -1:] - cumulative)
    own_state = jnp.einsum(
        "ushd,ushe->shde",
        k_local * jnp.transpose(remaining, (2, 0, 1))[..., None],
        v_local,
        precision=highest,
    )
    block_log = cumulative[..., -1]

    def combine(earlier, later_part):
        return (
            earlier[0] * later_part[0],
            later_part[0][..., None, None] * earlier[1] + later_part[1],
        )

    identity = (jnp.ones_like(block_log), jnp.zeros_like(own_state))
    _, prefix_state = entering((jnp.exp(block_log), own_state), "ctx", combine, identity)
    carried = jnp.exp(jnp.transpose(cumulative, (2, 0, 1)))[..., None] * jnp.einsum(
        "tshd,shde->tshe", q_local, prefix_state, precision=highest
    )
    heads_out = inside + carried
    mean_square = jnp.mean(heads_out * heads_out, axis=-1, keepdims=True)
    normed_heads = (
        heads_out * lax.rsqrt(mean_square + 1e-06) * attn_gain.reshape(head_count, head_size)
    )
    return normed_heads.astype(bf16).reshape(length * sequences, width)


def experts(rows, gate_weight, up_weight, down_weight):
    gate_out = jnp.dot(rows, gate_weight, preferred_element_type=f32)
    up_out = jnp.dot(rows, up_weight, preferred_element_type=f32)
    hidden = (silu_float(gate_out) * up_out).astype(bf16)
    return jnp.dot(hidden, down_weight, preferred_element_type=f32).astype(bf16)


def shards(
    queries,
    keys_in,
    values_in,
    log_decay,
    attn_gain,
    out_weight,
    residual,
    moe_gain,
    router,
    gate_weight,
    up_weight,
    down_weight,
    routes,
):
    n_ctx, n_ep = lax.axis_size("ctx"), lax.axis_size("ep")
    outer = 4
    fast = n_ep // outer
    high = n_ctx // fast
    place, member = lax.axis_index("ctx"), lax.axis_index("ep")
    far, near = member // fast, member % fast
    upper, lower = place // fast, place % fast
    model = residual.shape[-1]
    columns = out_weight.shape[1]

    def turned(a):
        pairs = []
        for h in range(high):
            for low in range(fast):
                for o in range(outer):
                    for n in range(fast):
                        source = (h * fast + low) * n_ep + o * fast + n
                        pairs.append((source, ((h ^ a) * fast + n) * n_ep + o * fast + low))
        return lax.ppermute(out_weight, ("ctx", "ep"), pairs)

    pieces = []
    for a in range(high):
        mine = turned(a)
        pieces.append(
            jnp.concatenate([mine] + [swap(mine, "ctx", j) for j in range(1, fast)], axis=0)
        )

    token_count = residual.shape[0] * residual.shape[1]
    own_residual = residual.reshape(token_count, model)
    own_routes = routes.reshape(token_count, 2)
    near_residual = absolute(
        [own_residual] + [swap(own_residual, "ep", k) for k in range(1, fast)], near
    )
    near_routes = absolute([own_routes] + [swap(own_routes, "ep", k) for k in range(1, fast)], near)

    normed_heads = attention(queries, keys_in, values_in, log_decay, attn_gain)
    heads = jnp.stack([normed_heads] + [swap(normed_heads, "ep", k) for k in range(1, fast)])
    heads = jnp.concatenate(
        [
            lax.dynamic_index_in_dim(heads, lower ^ j ^ near, 0, False)
            for j in range(fast)
        ],
        axis=1,
    ).reshape(outer, fast * token_count, -1)
    part = lambda k: lax.dynamic_index_in_dim(heads, far ^ k, 0, False)
    kept = jnp.concatenate([part(0), part(2)])
    given = jnp.concatenate([part(1), part(3)])
    block = fast * token_count
    attn = []
    for a in range(high):
        sent = jnp.dot(given, pieces[a], preferred_element_type=f32).astype(bf16)
        came = swap(sent, "ep", fast)
        total = jnp.dot(kept, pieces[a], preferred_element_type=f32) + came.astype(f32)
        came = swap(total[block:].astype(bf16), "ep", 2 * fast)
        total = total[:block] + came.astype(f32)
        narrow = total.astype(bf16)
        attn.extend([total] + [swap(narrow, "ep", k).astype(f32) for k in range(1, fast)])
    attn = absolute(attn, upper * fast + near)
    hidden_state = jnp.concatenate(near_residual).astype(f32) + jnp.concatenate(attn, axis=1)

    scale = lax.rsqrt(jnp.mean(hidden_state * hidden_state, axis=-1, keepdims=True) + 1e-06)
    moe_in = (hidden_state * scale * moe_gain).astype(bf16)
    logits = jnp.dot(moe_in, router, preferred_element_type=f32)
    expert_count = router.shape[1]
    capacity = max(2, 3 * token_count // expert_count)
    expert_ids = jnp.stack(near_routes)
    route_hot = expert_ids[..., None] == jnp.arange(expert_count, dtype=jnp.int32)
    picked = jnp.sum(
        jnp.where(route_hot, logits.reshape(fast, token_count, 1, expert_count), 0.0), axis=-1
    )
    weights = jax.nn.sigmoid(picked - picked[..., ::-1])
    hot_flat = route_hot.reshape(fast, 2 * token_count, expert_count).astype(jnp.int32)
    earlier = jnp.cumsum(hot_flat, axis=1) - hot_flat
    slots = jnp.sum(earlier * hot_flat, axis=-1).reshape(fast, token_count, 2)
    group = fast * capacity
    source = jnp.arange(fast, dtype=jnp.int32)[:, None, None]
    target = ((expert_ids // fast) ^ far) * group + source * capacity + slots
    target = jnp.where(expert_ids % fast == near, target, -1).reshape(block, 2)
    hit = target[..., None] == jnp.arange(outer * group, dtype=jnp.int32)
    placement = jnp.any(hit, axis=1).astype(bf16)
    mixing = jnp.sum(jnp.where(hit, weights.reshape(block, 2, 1), 0.0), axis=1)
    mixing_high = mixing.astype(bf16)
    mixing = jnp.concatenate([mixing_high, (mixing - mixing_high.astype(f32)).astype(bf16)])

    outgoing = jnp.dot(placement.T, moe_in, preferred_element_type=f32).astype(bf16)
    arrived = [outgoing[:group]] + [
        swap(outgoing[k * group : (k + 1) * group], "ep", k * fast) for k in range(1, outer)
    ]
    blocks = n_ctx // 2
    total = 0.0
    for first in (0, 2):
        own = jnp.concatenate(arrived[first : first + 2])
        size = own.shape[0]
        chip = jnp.concatenate([own] + [swap(own, "ctx", 2 * b) for b in range(1, blocks)])
        rows = jnp.concatenate([chip, swap(chip, "ctx", 1)])
        partial = experts(rows, gate_weight[0], up_weight[0], down_weight[0])
        half = blocks * size
        summed = partial[:half].astype(f32) + swap(partial[half:], "ctx", 1).astype(f32)
        result = summed[:size]
        for b in range(1, blocks):
            result = result + swap(
                summed[b * size : (b + 1) * size].astype(bf16), "ctx", 2 * b
            ).astype(f32)
        result = result.astype(bf16)
        returned = []
        for i, k in enumerate((first, first + 1)):
            piece = result[i * group : (i + 1) * group]
            returned.append(swap(piece, "ep", k * fast) if k else piece)
        returned = jnp.concatenate(returned)
        share = jnp.dot(
            mixing[:, first * group : (first + 2) * group], returned, preferred_element_type=f32
        )
        total = total + share[:block] + share[block:]
    total = total.reshape(fast, token_count, model)
    own_state = lax.dynamic_index_in_dim(
        hidden_state.reshape(fast, token_count, model), near, 0, False
    )
    result = own_state + lax.dynamic_index_in_dim(total, near, 0, False)
    for k in range(1, fast):
        other = lax.dynamic_index_in_dim(total, near ^ k, 0, False).astype(bf16)
        result = result + swap(other, "ep", k).astype(f32)
    return result.astype(bf16).reshape(residual.shape)


def solution(mesh):
    return jax.shard_map(
        shards,
        mesh=mesh,
        in_specs=(
            P("ctx", None, "ep"),
            P("ctx", None, "ep"),
            P("ctx", None, "ep"),
            P("ep", None, "ctx"),
            P("ep"),
            P("ep", "ctx"),
            P(("ctx", "ep"), None, None),
            P(),
            P(),
            P("ep", None, "ctx"),
            P("ep", None, "ctx"),
            P("ep", "ctx", None),
            P(("ctx", "ep"), None, None),
        ),
        out_specs=P(("ctx", "ep"), None, None),
        check_vma=False,
    )
```

```python
import functools
import jax
import jax.numpy as jnp
from jax import lax
from jax.experimental import pallas as pl
from jax.experimental.pallas import tpu as pltpu
from jax.sharding import PartitionSpec as P

highest = lax.Precision.HIGHEST
f32, bf16 = jnp.float32, jnp.bfloat16


def silu_float(values):
    return values * jax.nn.sigmoid(values)


def swap(array, axis, mask):
    size = lax.axis_size(axis)
    return lax.ppermute(array, axis, [(i, i ^ mask) for i in range(size)])


def absolute(items, me):
    items, bit = list(items), 1
    while bit < len(items):
        flip = (me & bit) != 0
        items = [jnp.where(flip, items[i ^ bit], items[i]) for i in range(len(items))]
        bit *= 2
    return items


TAIL = 16


def dot_highest(left, right, contract):
    return lax.dot_general(
        left, right, ((contract[:1], contract[1:]), ((), ())),
        precision=highest, preferred_element_type=f32,
    )


def within_kernel(heads, size, q_ref, k_ref, v_ref, decay_ref, inside_ref, query_ref, state_ref):
    length = q_ref.shape[0]
    row = lax.broadcasted_iota(jnp.int32, (length, length), 0)
    column = lax.broadcasted_iota(jnp.int32, (length, length), 1)
    causal = row >= column
    upto = jnp.where(causal, 1.0, 0.0).astype(f32)
    decay = decay_ref[...]
    along = dot_highest(decay, upto, (1, 1))
    down = dot_highest(upto, decay, (1, 1))
    for h in range(heads):
        span = slice(h * size, (h + 1) * size)
        query = silu_float(q_ref[:, span].astype(f32))
        key = silu_float(k_ref[:, span].astype(f32))
        value = v_ref[:, span].astype(f32)
        passed = down[:, h : h + 1]
        spacing = passed - along[h : h + 1, :]
        damping = jnp.where(causal, jnp.exp(jnp.where(causal, spacing, 0.0)), 0.0)
        scores = dot_highest(query, key, (1, 1)) * damping
        inside_ref[:, span] = dot_highest(scores, value, (1, 0))
        query_ref[:, span] = query * jnp.exp(passed)
        whole = passed[length - 1 : length, :]
        state = dot_highest(key * jnp.exp(whole - passed), value, (0, 0))
        base = h * (size + TAIL)
        state_ref[base : base + size, :] = state.astype(bf16)
        state_ref[base + size : base + size + TAIL, :] = jnp.broadcast_to(
            jnp.exp(whole), (TAIL, size)
        ).astype(bf16)


def across_kernel(heads, size, place_ref, states_ref, inside_ref, query_ref, gain_ref, out_ref):
    place = place_ref[0]
    for h in range(heads):
        span = slice(h * size, (h + 1) * size)
        base = h * (size + TAIL)
        state = jnp.zeros((size, size), f32)
        for hop in range(states_ref.shape[0]):
            own = states_ref[hop, base : base + size, :].astype(f32)
            decay = states_ref[hop, base + size : base + size + TAIL, :].astype(f32)[:1]
            state = jnp.where(hop < place, decay * state + own, state)
        total = inside_ref[:, span] + dot_highest(query_ref[:, span], state, (1, 0))
        mean_square = jnp.mean(total * total, axis=-1, keepdims=True)
        out_ref[:, span] = (
            total * lax.rsqrt(mean_square + 1e-06) * gain_ref[:, span]
        ).astype(bf16)


def attention(queries, keys_in, values_in, log_decay, attn_gain):
    length, sequences, width = queries.shape
    heads = log_decay.shape[0]
    size = width // heads
    flat = lambda a: a.reshape(length * sequences, width)
    inside, query, state = pl.pallas_call(
        functools.partial(within_kernel, heads, size),
        out_shape=(
            jax.ShapeDtypeStruct((length, width), f32),
            jax.ShapeDtypeStruct((length, width), f32),
            jax.ShapeDtypeStruct((heads * (size + TAIL), size), bf16),
        ),
        name="within_block",
    )(flat(queries), flat(keys_in), flat(values_in), log_decay.reshape(heads, length))
    states = lax.all_gather(state, "ctx")
    place = lax.axis_index("ctx").astype(jnp.int32).reshape(1)
    vmem = pl.BlockSpec(memory_space=pltpu.VMEM)
    return pl.pallas_call(
        functools.partial(across_kernel, heads, size),
        in_specs=[pl.BlockSpec(memory_space=pltpu.SMEM)] + [vmem] * 4,
        out_specs=vmem,
        out_shape=jax.ShapeDtypeStruct((length, width), bf16),
        name="across_blocks",
    )(place, states, inside, query, attn_gain.reshape(1, width))


def experts(rows, gate_weight, up_weight, down_weight):
    gate_out = jnp.dot(rows, gate_weight, preferred_element_type=f32)
    up_out = jnp.dot(rows, up_weight, preferred_element_type=f32)
    hidden = (silu_float(gate_out) * up_out).astype(bf16)
    return jnp.dot(hidden, down_weight, preferred_element_type=f32).astype(bf16)


def shards(
    queries,
    keys_in,
    values_in,
    log_decay,
    attn_gain,
    out_weight,
    residual,
    moe_gain,
    router,
    gate_weight,
    up_weight,
    down_weight,
    routes,
):
    n_ctx, n_ep = lax.axis_size("ctx"), lax.axis_size("ep")
    outer = 4
    fast = n_ep // outer
    high = n_ctx // fast
    place, member = lax.axis_index("ctx"), lax.axis_index("ep")
    far, near = member // fast, member % fast
    upper, lower = place // fast, place % fast
    model = residual.shape[-1]
    columns = out_weight.shape[1]

    def turned(a):
        pairs = []
        for h in range(high):
            for low in range(fast):
                for o in range(outer):
                    for n in range(fast):
                        source = (h * fast + low) * n_ep + o * fast + n
                        pairs.append((source, ((h ^ a) * fast + n) * n_ep + o * fast + low))
        return lax.ppermute(out_weight, ("ctx", "ep"), pairs)

    pieces = []
    for a in range(high):
        mine = turned(a)
        pieces.append(
            jnp.concatenate([mine] + [swap(mine, "ctx", j) for j in range(1, fast)], axis=0)
        )

    token_count = residual.shape[0] * residual.shape[1]
    own_residual = residual.reshape(token_count, model)
    own_routes = routes.reshape(token_count, 2)
    normed_heads = attention(queries, keys_in, values_in, log_decay, attn_gain)
    heads = jnp.stack([normed_heads] + [swap(normed_heads, "ep", k) for k in range(1, fast)])
    own_residual, own_routes, _ = lax.optimization_barrier((own_residual, own_routes, heads))
    near_residual = [own_residual] + [swap(own_residual, "ep", k) for k in range(1, fast)]
    near_routes = [own_routes] + [swap(own_routes, "ep", k) for k in range(1, fast)]
    heads = jnp.concatenate(
        [
            lax.dynamic_index_in_dim(heads, lower ^ j ^ near, 0, False)
            for j in range(fast)
        ],
        axis=1,
    ).reshape(outer, fast * token_count, -1)
    part = lambda k: lax.dynamic_index_in_dim(heads, far ^ k, 0, False)
    kept = jnp.concatenate([part(0), part(2)])
    given = jnp.concatenate([part(1), part(3)])
    block = fast * token_count
    attn = []
    for a in range(high):
        sent = jnp.dot(given, pieces[a], preferred_element_type=f32).astype(bf16)
        came = swap(sent, "ep", fast)
        if a == 0:
            near_routes, near_residual, came = lax.optimization_barrier(
                (near_routes, near_residual, came)
            )
            near_routes = absolute(near_routes, near)
            near_residual = absolute(near_residual, near)
        total = jnp.dot(kept, pieces[a], preferred_element_type=f32) + came.astype(f32)
        came = swap(total[block:].astype(bf16), "ep", 2 * fast)
        total = total[:block] + came.astype(f32)
        narrow = total.astype(bf16)
        attn.extend([total] + [swap(narrow, "ep", k).astype(f32) for k in range(1, fast)])
    attn = absolute(attn, upper * fast + near)
    hidden_state = jnp.concatenate(near_residual).astype(f32) + jnp.concatenate(attn, axis=1)

    scale = lax.rsqrt(jnp.mean(hidden_state * hidden_state, axis=-1, keepdims=True) + 1e-06)
    moe_in = (hidden_state * scale * moe_gain).astype(bf16)
    logits = jnp.dot(moe_in, router, preferred_element_type=f32)
    expert_count = router.shape[1]
    capacity = max(2, 3 * token_count // expert_count)
    expert_ids = jnp.stack(near_routes)
    route_hot = expert_ids[..., None] == jnp.arange(expert_count, dtype=jnp.int32)
    picked = jnp.sum(
        jnp.where(route_hot, logits.reshape(fast, token_count, 1, expert_count), 0.0), axis=-1
    )
    weights = jax.nn.sigmoid(picked - picked[..., ::-1])
    hot_flat = route_hot.reshape(fast, 2 * token_count, expert_count).astype(jnp.int32)
    earlier = jnp.cumsum(hot_flat, axis=1) - hot_flat
    slots = jnp.sum(earlier * hot_flat, axis=-1).reshape(fast, token_count, 2)
    group = fast * capacity
    source = jnp.arange(fast, dtype=jnp.int32)[:, None, None]
    target = ((expert_ids // fast) ^ far) * group + source * capacity + slots
    target = jnp.where(expert_ids % fast == near, target, -1).reshape(block, 2)
    hit = target[..., None] == jnp.arange(outer * group, dtype=jnp.int32)
    placement = jnp.any(hit, axis=1).astype(bf16)
    mixing = jnp.sum(jnp.where(hit, weights.reshape(block, 2, 1), 0.0), axis=1)

    outgoing = jnp.dot(placement.T, moe_in, preferred_element_type=f32).astype(bf16)
    arrived = [outgoing[k * group : (k + 1) * group] for k in range(outer)]
    for k in (2, 1):
        arrived[k] = swap(arrived[k], "ep", k * fast)
    arrived[3], _ = lax.optimization_barrier((arrived[3], arrived[1]))
    arrived[3] = swap(arrived[3], "ep", 3 * fast)
    blocks = n_ctx // 2
    over = [[swap(rows, "ctx", 2 * b) for b in range(1, blocks)] for rows in arrived]

    def visit(members, sooner, latest):
        chip = [arrived[k] for k in members]
        chip += [over[k][b] for b in range(blocks - 1) for k in members]
        chip, _ = lax.optimization_barrier((chip, sooner))
        chip = jnp.concatenate(chip)
        rows = jnp.concatenate([chip, swap(chip, "ctx", 1)])
        rows, _ = lax.optimization_barrier((rows, latest))
        partial = experts(rows, gate_weight[0], up_weight[0], down_weight[0])
        half = chip.shape[0]
        return partial[:half].astype(f32) + swap(partial[half:], "ctx", 1).astype(f32), partial

    def collect(summed, first, last):
        size = summed.shape[0] // blocks
        result = summed[first:last]
        for b in range(1, blocks):
            other = summed[b * size + first : b * size + last].astype(bf16)
            result = result + swap(other, "ctx", 2 * b).astype(f32)
        return result.astype(bf16)

    summed, partial = visit((0, 1), (), (arrived[2], arrived[3]))
    both = collect(summed, 0, 2 * group)
    summed, _ = visit((2, 3), partial, ())
    summed, both = lax.optimization_barrier((summed, both))
    returned = [both[:group], swap(both[group:], "ep", fast), None, None]
    third = collect(summed, group, 2 * group)
    summed, third = lax.optimization_barrier((summed, third))
    returned[3] = swap(third, "ep", 3 * fast)
    returned[2] = swap(collect(summed, 0, group), "ep", 2 * fast)

    def weighted(shares, rows):
        high = shares.astype(bf16)
        low = (shares - high.astype(f32)).astype(bf16)
        out = jnp.dot(jnp.concatenate([high, low]), rows, preferred_element_type=f32)
        return out[: shares.shape[0]] + out[shares.shape[0] :]

    cut = lambda k: mixing[:, k * group : (k + 1) * group]
    total = weighted(
        jnp.concatenate([cut(0), cut(1), cut(3)], axis=1),
        jnp.concatenate([returned[0], returned[1], returned[3]]),
    )
    mine = lambda a: lax.dynamic_index_in_dim(
        a.reshape((fast, token_count) + a.shape[1:]), near, 0, False
    )
    result = mine(hidden_state) + mine(total)
    shares, rows = [mine(cut(2))], [returned[2]]
    own_ids, own_slots, own_weights = mine(expert_ids.reshape(block, 2)), mine(slots.reshape(block, 2)), mine(weights.reshape(block, 2))
    for k in range(1, fast):
        other = lax.dynamic_index_in_dim(
            total.reshape(fast, token_count, model), near ^ k, 0, False
        )
        result = result + swap(other.astype(bf16), "ep", k).astype(f32)
        theirs = lax.dynamic_slice_in_dim(returned[2], (near ^ k) * capacity, capacity, 0)
        rows.append(swap(theirs, "ep", k))
        named = own_ids == (far ^ 2) * fast + (near ^ k)
        there = named[..., None] & (
            own_slots[..., None] == jnp.arange(capacity, dtype=jnp.int32)
        )
        shares.append(jnp.sum(jnp.where(there, own_weights[..., None], 0.0), axis=1))
    result = result + weighted(jnp.concatenate(shares, axis=1), jnp.concatenate(rows))
    return result.astype(bf16).reshape(residual.shape)


def solution(mesh):
    return jax.shard_map(
        shards,
        mesh=mesh,
        in_specs=(
            P("ctx", None, "ep"),
            P("ctx", None, "ep"),
            P("ctx", None, "ep"),
            P("ep", None, "ctx"),
            P("ep"),
            P("ep", "ctx"),
            P(("ctx", "ep"), None, None),
            P(),
            P(),
            P("ep", None, "ctx"),
            P("ep", None, "ctx"),
            P("ep", "ctx", None),
            P(("ctx", "ep"), None, None),
        ),
        out_specs=P(("ctx", "ep"), None, None),
        check_vma=False,
    )
```

```python
import functools
import jax
import jax.numpy as jnp
from jax import lax
from jax.experimental import pallas as pl
from jax.experimental.pallas import tpu as pltpu
from jax.sharding import PartitionSpec as P

highest = lax.Precision.HIGHEST
f32, bf16 = jnp.float32, jnp.bfloat16


def silu_float(values):
    return values * jax.nn.sigmoid(values)


def swap(array, axis, mask):
    size = lax.axis_size(axis)
    return lax.ppermute(array, axis, [(i, i ^ mask) for i in range(size)])


def absolute(items, me):
    items, bit = list(items), 1
    while bit < len(items):
        flip = (me & bit) != 0
        items = [jnp.where(flip, items[i ^ bit], items[i]) for i in range(len(items))]
        bit *= 2
    return items


TAIL = 16


def dot_highest(left, right, contract):
    return lax.dot_general(
        left, right, ((contract[:1], contract[1:]), ((), ())),
        precision=highest, preferred_element_type=f32,
    )


def within_kernel(heads, size, q_ref, k_ref, v_ref, decay_ref, inside_ref, query_ref, state_ref):
    length = q_ref.shape[0]
    row = lax.broadcasted_iota(jnp.int32, (length, length), 0)
    column = lax.broadcasted_iota(jnp.int32, (length, length), 1)
    causal = row >= column
    upto = jnp.where(causal, 1.0, 0.0).astype(f32)
    decay = decay_ref[...]
    along = dot_highest(decay, upto, (1, 1))
    down = dot_highest(upto, decay, (1, 1))
    for h in range(heads):
        span = slice(h * size, (h + 1) * size)
        query = silu_float(q_ref[:, span].astype(f32))
        key = silu_float(k_ref[:, span].astype(f32))
        value = v_ref[:, span].astype(f32)
        passed = down[:, h : h + 1]
        spacing = passed - along[h : h + 1, :]
        damping = jnp.where(causal, jnp.exp(jnp.where(causal, spacing, 0.0)), 0.0)
        scores = dot_highest(query, key, (1, 1)) * damping
        inside_ref[:, span] = dot_highest(scores, value, (1, 0))
        query_ref[:, span] = query * jnp.exp(passed)
        whole = passed[length - 1 : length, :]
        state = dot_highest(key * jnp.exp(whole - passed), value, (0, 0))
        base = h * (size + TAIL)
        state_ref[base : base + size, :] = state.astype(bf16)
        state_ref[base + size : base + size + TAIL, :] = jnp.broadcast_to(
            jnp.exp(whole), (TAIL, size)
        ).astype(bf16)


def across_kernel(heads, size, place_ref, states_ref, inside_ref, query_ref, gain_ref, out_ref):
    place = place_ref[0]
    for h in range(heads):
        span = slice(h * size, (h + 1) * size)
        base = h * (size + TAIL)
        state = jnp.zeros((size, size), f32)
        for hop in range(states_ref.shape[0]):
            own = states_ref[hop, base : base + size, :].astype(f32)
            decay = states_ref[hop, base + size : base + size + TAIL, :].astype(f32)[:1]
            state = jnp.where(hop < place, decay * state + own, state)
        total = inside_ref[:, span] + dot_highest(query_ref[:, span], state, (1, 0))
        mean_square = jnp.mean(total * total, axis=-1, keepdims=True)
        out_ref[:, span] = (
            total * lax.rsqrt(mean_square + 1e-06) * gain_ref[:, span]
        ).astype(bf16)


def attention(queries, keys_in, values_in, log_decay, attn_gain, beside):
    length, sequences, width = queries.shape
    heads = log_decay.shape[0]
    size = width // heads
    flat = lambda a: a.reshape(length * sequences, width)
    inside, query, state = pl.pallas_call(
        functools.partial(within_kernel, heads, size),
        out_shape=(
            jax.ShapeDtypeStruct((length, width), f32),
            jax.ShapeDtypeStruct((length, width), f32),
            jax.ShapeDtypeStruct((heads * (size + TAIL), size), bf16),
        ),
        name="within_block",
    )(flat(queries), flat(keys_in), flat(values_in), log_decay.reshape(heads, length))
    states, beside = lax.optimization_barrier((lax.all_gather(state, "ctx"), beside))
    place = lax.axis_index("ctx").astype(jnp.int32).reshape(1)
    vmem = pl.BlockSpec(memory_space=pltpu.VMEM)
    return pl.pallas_call(
        functools.partial(across_kernel, heads, size),
        in_specs=[pl.BlockSpec(memory_space=pltpu.SMEM)] + [vmem] * 4,
        out_specs=vmem,
        out_shape=jax.ShapeDtypeStruct((length, width), bf16),
        name="across_blocks",
    )(place, states, inside, query, attn_gain.reshape(1, width)), beside


def experts(rows, gate_weight, up_weight, down_weight):
    gate_out = jnp.dot(rows, gate_weight, preferred_element_type=f32)
    up_out = jnp.dot(rows, up_weight, preferred_element_type=f32)
    hidden = (silu_float(gate_out) * up_out).astype(bf16)
    return jnp.dot(hidden, down_weight, preferred_element_type=f32).astype(bf16)


def shards(
    queries,
    keys_in,
    values_in,
    log_decay,
    attn_gain,
    out_weight,
    residual,
    moe_gain,
    router,
    gate_weight,
    up_weight,
    down_weight,
    routes,
):
    n_ctx, n_ep = lax.axis_size("ctx"), lax.axis_size("ep")
    outer = 4
    fast = n_ep // outer
    high = n_ctx // fast
    place, member = lax.axis_index("ctx"), lax.axis_index("ep")
    far, near = member // fast, member % fast
    upper, lower = place // fast, place % fast
    model = residual.shape[-1]
    columns = out_weight.shape[1]

    def turned(rows, a):
        pairs = []
        for h in range(high):
            for low in range(fast):
                for o in range(outer):
                    for n in range(fast):
                        source = (h * fast + low) * n_ep + o * fast + n
                        goal = ((h ^ a) * fast + n) * n_ep + o * fast + low
                        if source != goal:
                            pairs.append((source, goal))
        return lax.ppermute(rows, ("ctx", "ep"), pairs)

    soon = [turned(out_weight, a) for a in range(high)]

    token_count = residual.shape[0] * residual.shape[1]
    own_residual = residual.reshape(token_count, model)
    own_routes = routes.reshape(token_count, 2)
    normed_heads, soon = attention(queries, keys_in, values_in, log_decay, attn_gain, soon)
    soon[0] = jnp.where(lower == near, out_weight, soon[0])
    pieces = [
        jnp.concatenate([mine] + [swap(mine, "ctx", j) for j in range(1, fast)], axis=0)
        for mine in soon
    ]
    heads = jnp.stack([normed_heads] + [swap(normed_heads, "ep", k) for k in range(1, fast)])
    own_residual, own_routes, heads = lax.optimization_barrier((own_residual, own_routes, heads))
    near_residual = [own_residual] + [swap(own_residual, "ep", k) for k in range(1, fast)]
    near_routes = [own_routes] + [swap(own_routes, "ep", k) for k in range(1, fast)]
    heads = jnp.concatenate(
        [
            lax.dynamic_index_in_dim(heads, lower ^ j ^ near, 0, False)
            for j in range(fast)
        ],
        axis=1,
    ).reshape(outer, fast * token_count, -1)
    part = lambda k: lax.dynamic_index_in_dim(heads, far ^ k, 0, False)
    kept = jnp.concatenate([part(0), part(2)])
    given = jnp.concatenate([part(1), part(3)])
    block = fast * token_count
    attn = []
    for a in range(high):
        sent = jnp.dot(given, pieces[a], preferred_element_type=f32).astype(bf16)
        came = swap(sent, "ep", fast)
        if a == 0:
            near_routes, near_residual, came = lax.optimization_barrier(
                (near_routes, near_residual, came)
            )
            near_routes = absolute(near_routes, near)
            near_residual = absolute(near_residual, near)
        else:
            came, earlier = lax.optimization_barrier((came, earlier))
        total = jnp.dot(kept, pieces[a], preferred_element_type=f32) + came.astype(f32)
        came = swap(total[block:].astype(bf16), "ep", 2 * fast)
        earlier = came
        total = total[:block] + came.astype(f32)
        narrow = total.astype(bf16)
        attn.extend([total] + [swap(narrow, "ep", k).astype(f32) for k in range(1, fast)])
    attn = absolute(attn, upper * fast + near)
    hidden_state = jnp.concatenate(near_residual).astype(f32) + jnp.concatenate(attn, axis=1)

    scale = lax.rsqrt(jnp.mean(hidden_state * hidden_state, axis=-1, keepdims=True) + 1e-06)
    moe_in = (hidden_state * scale * moe_gain).astype(bf16)
    logits = jnp.dot(moe_in, router, preferred_element_type=f32)
    expert_count = router.shape[1]
    capacity = max(2, 3 * token_count // expert_count)
    expert_ids = jnp.stack(near_routes)
    route_hot = expert_ids[..., None] == jnp.arange(expert_count, dtype=jnp.int32)
    picked = jnp.sum(
        jnp.where(route_hot, logits.reshape(fast, token_count, 1, expert_count), 0.0), axis=-1
    )
    weights = jax.nn.sigmoid(picked - picked[..., ::-1])
    hot_flat = route_hot.reshape(fast, 2 * token_count, expert_count).astype(jnp.int32)
    earlier = jnp.cumsum(hot_flat, axis=1) - hot_flat
    slots = jnp.sum(earlier * hot_flat, axis=-1).reshape(fast, token_count, 2)
    group = fast * capacity
    source = jnp.arange(fast, dtype=jnp.int32)[:, None, None]
    target = ((expert_ids // fast) ^ far) * group + source * capacity + slots
    target = jnp.where(expert_ids % fast == near, target, -1).reshape(block, 2)
    hit = target[..., None] == jnp.arange(outer * group, dtype=jnp.int32)
    placement = jnp.any(hit, axis=1).astype(bf16)
    mixing = jnp.sum(jnp.where(hit, weights.reshape(block, 2, 1), 0.0), axis=1)

    outgoing = jnp.dot(placement.T, moe_in, preferred_element_type=f32).astype(bf16)
    arrived = [outgoing[k * group : (k + 1) * group] for k in range(outer)]
    for k in (2, 1):
        arrived[k] = swap(arrived[k], "ep", k * fast)
    arrived[3], _ = lax.optimization_barrier((arrived[3], arrived[1]))
    arrived[3] = swap(arrived[3], "ep", 3 * fast)
    blocks = n_ctx // 2
    over = [[swap(rows, "ctx", 2 * b) for b in range(1, blocks)] for rows in arrived]

    def visit(members, sooner, latest):
        chip = [arrived[k] for k in members]
        chip += [over[k][b] for b in range(blocks - 1) for k in members]
        chip, _ = lax.optimization_barrier((chip, sooner))
        chip = jnp.concatenate(chip)
        rows = jnp.concatenate([chip, swap(chip, "ctx", 1)])
        rows, _ = lax.optimization_barrier((rows, latest))
        partial = experts(rows, gate_weight[0], up_weight[0], down_weight[0])
        half = chip.shape[0]
        return partial[:half].astype(f32) + swap(partial[half:], "ctx", 1).astype(f32), partial

    def collect(summed, first, last):
        size = summed.shape[0] // blocks
        result = summed[first:last]
        for b in range(1, blocks):
            other = summed[b * size + first : b * size + last].astype(bf16)
            result = result + swap(other, "ctx", 2 * b).astype(f32)
        return result.astype(bf16)

    summed, partial = visit((0, 1), (), (arrived[2], arrived[3]))
    both = collect(summed, 0, 2 * group)
    summed, _ = visit((2, 3), partial, ())
    summed, both = lax.optimization_barrier((summed, both))
    returned = [both[:group], swap(both[group:], "ep", fast), None, None]
    third = collect(summed, group, 2 * group)
    summed, third = lax.optimization_barrier((summed, third))
    returned[3] = swap(third, "ep", 3 * fast)
    returned[2] = swap(collect(summed, 0, group), "ep", 2 * fast)

    def weighted(shares, rows):
        high = shares.astype(bf16)
        low = (shares - high.astype(f32)).astype(bf16)
        out = jnp.dot(jnp.concatenate([high, low]), rows, preferred_element_type=f32)
        return out[: shares.shape[0]] + out[shares.shape[0] :]

    cut = lambda k: mixing[:, k * group : (k + 1) * group]
    total = weighted(
        jnp.concatenate([cut(0), cut(1), cut(3)], axis=1),
        jnp.concatenate([returned[0], returned[1], returned[3]]),
    )
    mine = lambda a: lax.dynamic_index_in_dim(
        a.reshape((fast, token_count) + a.shape[1:]), near, 0, False
    )
    result = mine(hidden_state) + mine(total)
    shares, rows = [mine(cut(2))], [returned[2]]
    own_ids, own_slots, own_weights = mine(expert_ids.reshape(block, 2)), mine(slots.reshape(block, 2)), mine(weights.reshape(block, 2))
    for k in range(1, fast):
        other = lax.dynamic_index_in_dim(
            total.reshape(fast, token_count, model), near ^ k, 0, False
        )
        result = result + swap(other.astype(bf16), "ep", k).astype(f32)
        theirs = lax.dynamic_slice_in_dim(returned[2], (near ^ k) * capacity, capacity, 0)
        rows.append(swap(theirs, "ep", k))
        named = own_ids == (far ^ 2) * fast + (near ^ k)
        there = named[..., None] & (
            own_slots[..., None] == jnp.arange(capacity, dtype=jnp.int32)
        )
        shares.append(jnp.sum(jnp.where(there, own_weights[..., None], 0.0), axis=1))
    result = result + weighted(jnp.concatenate(shares, axis=1), jnp.concatenate(rows))
    return result.astype(bf16).reshape(residual.shape)


def solution(mesh):
    return jax.shard_map(
        shards,
        mesh=mesh,
        in_specs=(
            P("ctx", None, "ep"),
            P("ctx", None, "ep"),
            P("ctx", None, "ep"),
            P("ep", None, "ctx"),
            P("ep"),
            P("ep", "ctx"),
            P(("ctx", "ep"), None, None),
            P(),
            P(),
            P("ep", None, "ctx"),
            P("ep", None, "ctx"),
            P("ep", "ctx", None),
            P(("ctx", "ep"), None, None),
        ),
        out_specs=P(("ctx", "ep"), None, None),
        check_vma=False,
    )
```

```python
import functools
import jax
import jax.numpy as jnp
from jax import lax
from jax.experimental import pallas as pl
from jax.experimental.pallas import tpu as pltpu
from jax.sharding import PartitionSpec as P

highest = lax.Precision.HIGHEST
f32, bf16 = jnp.float32, jnp.bfloat16


def silu_float(values):
    return values * jax.nn.sigmoid(values)


def swap(array, axis, mask):
    size = lax.axis_size(axis)
    return lax.ppermute(array, axis, [(i, i ^ mask) for i in range(size)])


def absolute(items, me):
    items, bit = list(items), 1
    while bit < len(items):
        flip = (me & bit) != 0
        items = [jnp.where(flip, items[i ^ bit], items[i]) for i in range(len(items))]
        bit *= 2
    return items


TAIL = 16


def dot_highest(left, right, contract):
    return lax.dot_general(
        left, right, ((contract[:1], contract[1:]), ((), ())),
        precision=highest, preferred_element_type=f32,
    )


def within_kernel(heads, size, q_ref, k_ref, v_ref, decay_ref, inside_ref, query_ref, state_ref):
    length = q_ref.shape[0]
    row = lax.broadcasted_iota(jnp.int32, (length, length), 0)
    column = lax.broadcasted_iota(jnp.int32, (length, length), 1)
    causal = row >= column
    upto = jnp.where(causal, 1.0, 0.0).astype(f32)
    decay = decay_ref[...]
    along = dot_highest(decay, upto, (1, 1))
    down = dot_highest(upto, decay, (1, 1))
    for h in range(heads):
        span = slice(h * size, (h + 1) * size)
        query = silu_float(q_ref[:, span].astype(f32))
        key = silu_float(k_ref[:, span].astype(f32))
        value = v_ref[:, span].astype(f32)
        passed = down[:, h : h + 1]
        spacing = passed - along[h : h + 1, :]
        damping = jnp.where(causal, jnp.exp(jnp.where(causal, spacing, 0.0)), 0.0)
        scores = dot_highest(query, key, (1, 1)) * damping
        inside_ref[:, span] = dot_highest(scores, value, (1, 0))
        query_ref[:, span] = query * jnp.exp(passed)
        whole = passed[length - 1 : length, :]
        state = dot_highest(key * jnp.exp(whole - passed), value, (0, 0))
        base = h * (size + TAIL)
        state_ref[base : base + size, :] = state.astype(bf16)
        state_ref[base + size : base + size + TAIL, :] = jnp.broadcast_to(
            jnp.exp(whole), (TAIL, size)
        ).astype(bf16)


def across_kernel(heads, size, place_ref, states_ref, inside_ref, query_ref, gain_ref, out_ref):
    place = place_ref[0]
    for h in range(heads):
        span = slice(h * size, (h + 1) * size)
        base = h * (size + TAIL)
        state = jnp.zeros((size, size), f32)
        for hop in range(states_ref.shape[0]):
            own = states_ref[hop, base : base + size, :].astype(f32)
            decay = states_ref[hop, base + size : base + size + TAIL, :].astype(f32)[:1]
            state = jnp.where(hop < place, decay * state + own, state)
        total = inside_ref[:, span] + dot_highest(query_ref[:, span], state, (1, 0))
        mean_square = jnp.mean(total * total, axis=-1, keepdims=True)
        out_ref[:, span] = (
            total * lax.rsqrt(mean_square + 1e-06) * gain_ref[:, span]
        ).astype(bf16)


def attention(queries, keys_in, values_in, log_decay, attn_gain, beside):
    length, sequences, width = queries.shape
    heads = log_decay.shape[0]
    size = width // heads
    flat = lambda a: a.reshape(length * sequences, width)
    inside, query, state = pl.pallas_call(
        functools.partial(within_kernel, heads, size),
        out_shape=(
            jax.ShapeDtypeStruct((length, width), f32),
            jax.ShapeDtypeStruct((length, width), f32),
            jax.ShapeDtypeStruct((heads * (size + TAIL), size), bf16),
        ),
        name="within_block",
    )(flat(queries), flat(keys_in), flat(values_in), log_decay.reshape(heads, length))
    states, beside = lax.optimization_barrier((lax.all_gather(state, "ctx"), beside))
    place = lax.axis_index("ctx").astype(jnp.int32).reshape(1)
    vmem = pl.BlockSpec(memory_space=pltpu.VMEM)
    return pl.pallas_call(
        functools.partial(across_kernel, heads, size),
        in_specs=[pl.BlockSpec(memory_space=pltpu.SMEM)] + [vmem] * 4,
        out_specs=vmem,
        out_shape=jax.ShapeDtypeStruct((length, width), bf16),
        name="across_blocks",
    )(place, states, inside, query, attn_gain.reshape(1, width)), beside


def experts(rows, gate_weight, up_weight, down_weight):
    gate_out = jnp.dot(rows, gate_weight, preferred_element_type=f32)
    up_out = jnp.dot(rows, up_weight, preferred_element_type=f32)
    hidden = (silu_float(gate_out) * up_out).astype(bf16)
    return jnp.dot(hidden, down_weight, preferred_element_type=f32).astype(bf16)


def shards(
    queries,
    keys_in,
    values_in,
    log_decay,
    attn_gain,
    out_weight,
    residual,
    moe_gain,
    router,
    gate_weight,
    up_weight,
    down_weight,
    routes,
):
    n_ctx, n_ep = lax.axis_size("ctx"), lax.axis_size("ep")
    outer = 4
    fast = n_ep // outer
    high = n_ctx // fast
    place, member = lax.axis_index("ctx"), lax.axis_index("ep")
    far, near = member // fast, member % fast
    upper, lower = place // fast, place % fast
    model = residual.shape[-1]
    columns = out_weight.shape[1]

    def turned(rows, a):
        pairs = []
        for h in range(high):
            for low in range(fast):
                for o in range(outer):
                    for n in range(fast):
                        source = (h * fast + low) * n_ep + o * fast + n
                        goal = ((h ^ a) * fast + n) * n_ep + o * fast + low
                        if source != goal:
                            pairs.append((source, goal))
        return lax.ppermute(rows, ("ctx", "ep"), pairs)

    soon = [turned(out_weight, a) for a in range(high)]

    token_count = residual.shape[0] * residual.shape[1]
    own_residual = residual.reshape(token_count, model)
    own_routes = routes.reshape(token_count, 2)
    normed_heads, soon = attention(queries, keys_in, values_in, log_decay, attn_gain, soon)
    soon[0] = jnp.where(lower == near, out_weight, soon[0])
    pieces = [
        jnp.concatenate([mine] + [swap(mine, "ctx", j) for j in range(1, fast)], axis=0)
        for mine in soon
    ]
    heads = jnp.stack([normed_heads] + [swap(normed_heads, "ep", k) for k in range(1, fast)])
    own_residual, own_routes, heads = lax.optimization_barrier((own_residual, own_routes, heads))
    near_residual = [own_residual] + [swap(own_residual, "ep", k) for k in range(1, fast)]
    near_routes = [own_routes] + [swap(own_routes, "ep", k) for k in range(1, fast)]
    heads = jnp.concatenate(
        [
            lax.dynamic_index_in_dim(heads, lower ^ j ^ near, 0, False)
            for j in range(fast)
        ],
        axis=1,
    ).reshape(outer, fast * token_count, -1)
    part = lambda k: lax.dynamic_index_in_dim(heads, far ^ k, 0, False)
    kept = jnp.concatenate([part(0), part(2)])
    given = jnp.concatenate([part(1), part(3)])
    block = fast * token_count
    attn = []
    for a in range(high):
        sent = jnp.dot(given, pieces[a], preferred_element_type=f32).astype(bf16)
        came = swap(sent, "ep", fast)
        if a == 0:
            near_routes, near_residual, came = lax.optimization_barrier(
                (near_routes, near_residual, came)
            )
            near_routes = absolute(near_routes, near)
            near_residual = absolute(near_residual, near)
        else:
            came, earlier = lax.optimization_barrier((came, earlier))
        total = jnp.dot(kept, pieces[a], preferred_element_type=f32) + came.astype(f32)
        came = swap(total[block:].astype(bf16), "ep", 2 * fast)
        earlier = came
        total = total[:block] + came.astype(f32)
        narrow = total.astype(bf16)
        attn.extend([total] + [swap(narrow, "ep", k).astype(f32) for k in range(1, fast)])
    attn = absolute(attn, upper * fast + near)
    hidden_state = jnp.concatenate(near_residual).astype(f32) + jnp.concatenate(attn, axis=1)

    scale = lax.rsqrt(jnp.mean(hidden_state * hidden_state, axis=-1, keepdims=True) + 1e-06)
    moe_in = (hidden_state * scale * moe_gain).astype(bf16)
    logits = jnp.dot(moe_in, router, preferred_element_type=f32)
    expert_count = router.shape[1]
    capacity = max(2, 3 * token_count // expert_count)
    expert_ids = jnp.stack(near_routes)
    route_hot = expert_ids[..., None] == jnp.arange(expert_count, dtype=jnp.int32)
    picked = jnp.sum(
        jnp.where(route_hot, logits.reshape(fast, token_count, 1, expert_count), 0.0), axis=-1
    )
    weights = jax.nn.sigmoid(picked - picked[..., ::-1])
    hot_flat = route_hot.reshape(fast, 2 * token_count, expert_count).astype(jnp.int32)
    earlier = jnp.cumsum(hot_flat, axis=1) - hot_flat
    slots = jnp.sum(earlier * hot_flat, axis=-1).reshape(fast, token_count, 2)
    group = fast * capacity
    source = jnp.arange(fast, dtype=jnp.int32)[:, None, None]
    target = ((expert_ids // fast) ^ far) * group + source * capacity + slots
    target = jnp.where(expert_ids % fast == near, target, -1).reshape(block, 2)
    hit = target[..., None] == jnp.arange(outer * group, dtype=jnp.int32)
    placement = jnp.any(hit, axis=1).astype(bf16)
    mixing = jnp.sum(jnp.where(hit, weights.reshape(block, 2, 1), 0.0), axis=1)

    outgoing = jnp.dot(placement.T, moe_in, preferred_element_type=f32).astype(bf16)
    arrived = [outgoing[k * group : (k + 1) * group] for k in range(outer)]
    for k in (2, 1):
        arrived[k] = swap(arrived[k], "ep", k * fast)
    arrived[3], _ = lax.optimization_barrier((arrived[3], arrived[1]))
    arrived[3] = swap(arrived[3], "ep", 3 * fast)
    blocks = n_ctx // 2
    over = [[swap(rows, "ctx", 2 * b) for b in range(1, blocks)] for rows in arrived]

    def visit(members, sooner, latest):
        chip = [arrived[k] for k in members]
        chip += [over[k][b] for b in range(blocks - 1) for k in members]
        chip, _ = lax.optimization_barrier((chip, sooner))
        chip = jnp.concatenate(chip)
        rows = jnp.concatenate([chip, swap(chip, "ctx", 1)])
        rows, _ = lax.optimization_barrier((rows, latest))
        partial = experts(rows, gate_weight[0], up_weight[0], down_weight[0])
        half = chip.shape[0]
        return partial[:half].astype(f32) + swap(partial[half:], "ctx", 1).astype(f32), partial

    def collect(summed, first, last):
        size = summed.shape[0] // blocks
        result = summed[first:last]
        for b in range(1, blocks):
            other = summed[b * size + first : b * size + last].astype(bf16)
            result = result + swap(other, "ctx", 2 * b).astype(f32)
        return result.astype(bf16)

    early, partial = visit((0, 1), (), (arrived[2], arrived[3]))
    second = collect(early, group, 2 * group)
    summed, _ = visit((2, 3), partial, ())
    summed, second = lax.optimization_barrier((summed, second))
    third = collect(summed, group, 2 * group)
    summed, early, third = lax.optimization_barrier((summed, early, third))
    returned = [
        collect(early, 0, group),
        swap(second, "ep", fast),
        swap(collect(summed, 0, group), "ep", 2 * fast),
        swap(third, "ep", 3 * fast),
    ]

    def weighted(shares, rows):
        high = shares.astype(bf16)
        low = (shares - high.astype(f32)).astype(bf16)
        out = jnp.dot(jnp.concatenate([high, low]), rows, preferred_element_type=f32)
        return out[: shares.shape[0]] + out[shares.shape[0] :]

    cut = lambda k: mixing[:, k * group : (k + 1) * group]
    total = weighted(
        jnp.concatenate([cut(0), cut(1), cut(3)], axis=1),
        jnp.concatenate([returned[0], returned[1], returned[3]]),
    )
    mine = lambda a: lax.dynamic_index_in_dim(
        a.reshape((fast, token_count) + a.shape[1:]), near, 0, False
    )
    result = mine(hidden_state) + mine(total)
    shares, rows = [mine(cut(2))], [returned[2]]
    own_ids, own_slots, own_weights = mine(expert_ids.reshape(block, 2)), mine(slots.reshape(block, 2)), mine(weights.reshape(block, 2))
    for k in range(1, fast):
        other = lax.dynamic_index_in_dim(
            total.reshape(fast, token_count, model), near ^ k, 0, False
        )
        result = result + swap(other.astype(bf16), "ep", k).astype(f32)
        theirs = lax.dynamic_slice_in_dim(returned[2], (near ^ k) * capacity, capacity, 0)
        rows.append(swap(theirs, "ep", k))
        named = own_ids == (far ^ 2) * fast + (near ^ k)
        there = named[..., None] & (
            own_slots[..., None] == jnp.arange(capacity, dtype=jnp.int32)
        )
        shares.append(jnp.sum(jnp.where(there, own_weights[..., None], 0.0), axis=1))
    result = result + weighted(jnp.concatenate(shares, axis=1), jnp.concatenate(rows))
    return result.astype(bf16).reshape(residual.shape)


def solution(mesh):
    return jax.shard_map(
        shards,
        mesh=mesh,
        in_specs=(
            P("ctx", None, "ep"),
            P("ctx", None, "ep"),
            P("ctx", None, "ep"),
            P("ep", None, "ctx"),
            P("ep"),
            P("ep", "ctx"),
            P(("ctx", "ep"), None, None),
            P(),
            P(),
            P("ep", None, "ctx"),
            P("ep", None, "ctx"),
            P("ep", "ctx", None),
            P(("ctx", "ep"), None, None),
        ),
        out_specs=P(("ctx", "ep"), None, None),
        check_vma=False,
    )
```

```python
import functools
import jax
import jax.numpy as jnp
from jax import lax
from jax.experimental import pallas as pl
from jax.experimental.pallas import tpu as pltpu
from jax.sharding import PartitionSpec as P

highest = lax.Precision.HIGHEST
f32, bf16 = jnp.float32, jnp.bfloat16


def silu_float(values):
    return values * jax.nn.sigmoid(values)


def swap(array, axis, mask):
    size = lax.axis_size(axis)
    return lax.ppermute(array, axis, [(i, i ^ mask) for i in range(size)])


def absolute(items, me):
    items, bit = list(items), 1
    while bit < len(items):
        flip = (me & bit) != 0
        items = [jnp.where(flip, items[i ^ bit], items[i]) for i in range(len(items))]
        bit *= 2
    return items


TAIL = 16


def dot_highest(left, right, contract):
    return lax.dot_general(
        left, right, ((contract[:1], contract[1:]), ((), ())),
        precision=highest, preferred_element_type=f32,
    )


def within_kernel(heads, size, q_ref, k_ref, v_ref, decay_ref, inside_ref, query_ref, state_ref):
    length = q_ref.shape[0]
    row = lax.broadcasted_iota(jnp.int32, (length, length), 0)
    column = lax.broadcasted_iota(jnp.int32, (length, length), 1)
    causal = row >= column
    upto = jnp.where(causal, 1.0, 0.0).astype(f32)
    decay = decay_ref[...]
    along = dot_highest(decay, upto, (1, 1))
    down = dot_highest(upto, decay, (1, 1))
    for h in range(heads):
        span = slice(h * size, (h + 1) * size)
        query = silu_float(q_ref[:, span].astype(f32))
        key = silu_float(k_ref[:, span].astype(f32))
        value = v_ref[:, span].astype(f32)
        passed = down[:, h : h + 1]
        spacing = passed - along[h : h + 1, :]
        damping = jnp.where(causal, jnp.exp(jnp.where(causal, spacing, 0.0)), 0.0)
        scores = dot_highest(query, key, (1, 1)) * damping
        inside_ref[:, span] = dot_highest(scores, value, (1, 0))
        query_ref[:, span] = query * jnp.exp(passed)
        whole = passed[length - 1 : length, :]
        state = dot_highest(key * jnp.exp(whole - passed), value, (0, 0))
        base = h * (size + TAIL)
        state_ref[base : base + size, :] = state.astype(bf16)
        state_ref[base + size : base + size + TAIL, :] = jnp.broadcast_to(
            jnp.exp(whole), (TAIL, size)
        ).astype(bf16)


def across_kernel(heads, size, place_ref, states_ref, inside_ref, query_ref, gain_ref, out_ref):
    place = place_ref[0]
    for h in range(heads):
        span = slice(h * size, (h + 1) * size)
        base = h * (size + TAIL)
        state = jnp.zeros((size, size), f32)
        for hop in range(states_ref.shape[0]):
            own = states_ref[hop, base : base + size, :].astype(f32)
            decay = states_ref[hop, base + size : base + size + TAIL, :].astype(f32)[:1]
            state = jnp.where(hop < place, decay * state + own, state)
        total = inside_ref[:, span] + dot_highest(query_ref[:, span], state, (1, 0))
        mean_square = jnp.mean(total * total, axis=-1, keepdims=True)
        out_ref[:, span] = (
            total * lax.rsqrt(mean_square + 1e-06) * gain_ref[:, span]
        ).astype(bf16)


def attention(queries, keys_in, values_in, log_decay, attn_gain, beside):
    length, sequences, width = queries.shape
    heads = log_decay.shape[0]
    size = width // heads
    flat = lambda a: a.reshape(length * sequences, width)
    inside, query, state = pl.pallas_call(
        functools.partial(within_kernel, heads, size),
        out_shape=(
            jax.ShapeDtypeStruct((length, width), f32),
            jax.ShapeDtypeStruct((length, width), f32),
            jax.ShapeDtypeStruct((heads * (size + TAIL), size), bf16),
        ),
        name="within_block",
    )(flat(queries), flat(keys_in), flat(values_in), log_decay.reshape(heads, length))
    states, beside = lax.optimization_barrier((lax.all_gather(state, "ctx"), beside))
    place = lax.axis_index("ctx").astype(jnp.int32).reshape(1)
    vmem = pl.BlockSpec(memory_space=pltpu.VMEM)
    return pl.pallas_call(
        functools.partial(across_kernel, heads, size),
        in_specs=[pl.BlockSpec(memory_space=pltpu.SMEM)] + [vmem] * 4,
        out_specs=vmem,
        out_shape=jax.ShapeDtypeStruct((length, width), bf16),
        name="across_blocks",
    )(place, states, inside, query, attn_gain.reshape(1, width)), beside


def experts(rows, gate_weight, up_weight, down_weight):
    gate_out = jnp.dot(rows, gate_weight, preferred_element_type=f32)
    up_out = jnp.dot(rows, up_weight, preferred_element_type=f32)
    hidden = (silu_float(gate_out) * up_out).astype(bf16)
    return jnp.dot(hidden, down_weight, preferred_element_type=f32).astype(bf16)


def shards(
    queries,
    keys_in,
    values_in,
    log_decay,
    attn_gain,
    out_weight,
    residual,
    moe_gain,
    router,
    gate_weight,
    up_weight,
    down_weight,
    routes,
):
    n_ctx, n_ep = lax.axis_size("ctx"), lax.axis_size("ep")
    outer = 4
    fast = n_ep // outer
    high = n_ctx // fast
    place, member = lax.axis_index("ctx"), lax.axis_index("ep")
    far, near = member // fast, member % fast
    upper, lower = place // fast, place % fast
    model = residual.shape[-1]
    columns = out_weight.shape[1]

    def turned(rows, a):
        pairs = []
        for h in range(high):
            for low in range(fast):
                for o in range(outer):
                    for n in range(fast):
                        source = (h * fast + low) * n_ep + o * fast + n
                        goal = ((h ^ a) * fast + n) * n_ep + o * fast + low
                        if source != goal:
                            pairs.append((source, goal))
        return lax.ppermute(rows, ("ctx", "ep"), pairs)

    soon = [turned(out_weight, a) for a in range(high)]

    token_count = residual.shape[0] * residual.shape[1]
    own_residual = residual.reshape(token_count, model)
    own_routes = routes.reshape(token_count, 2)
    normed_heads, soon = attention(queries, keys_in, values_in, log_decay, attn_gain, soon)
    soon[0] = jnp.where(lower == near, out_weight, soon[0])
    pieces = [
        jnp.concatenate([mine] + [swap(mine, "ctx", j) for j in range(1, fast)], axis=0)
        for mine in soon
    ]
    heads = jnp.stack([normed_heads] + [swap(normed_heads, "ep", k) for k in range(1, fast)])
    heads = jnp.concatenate(
        [
            lax.dynamic_index_in_dim(heads, lower ^ j ^ near, 0, False)
            for j in range(fast)
        ],
        axis=1,
    ).reshape(outer, fast * token_count, -1)
    part = lambda k: lax.dynamic_index_in_dim(heads, far ^ k, 0, False)
    kept = jnp.concatenate([part(0), part(2)])
    given = jnp.concatenate([part(1), part(3)])
    block = fast * token_count
    attn = []
    for a in range(high):
        sent = jnp.dot(given, pieces[a], preferred_element_type=f32).astype(bf16)
        if a == 0:
            own_residual, own_routes, sent = lax.optimization_barrier(
                (own_residual, own_routes, sent)
            )
            near_residual = [own_residual] + [swap(own_residual, "ep", k) for k in range(1, fast)]
            near_routes = [own_routes] + [swap(own_routes, "ep", k) for k in range(1, fast)]
        came = swap(sent, "ep", fast)
        if a == 0:
            near_routes, near_residual, came = lax.optimization_barrier(
                (near_routes, near_residual, came)
            )
            near_routes = absolute(near_routes, near)
            near_residual = absolute(near_residual, near)
        else:
            came, earlier = lax.optimization_barrier((came, earlier))
        total = jnp.dot(kept, pieces[a], preferred_element_type=f32) + came.astype(f32)
        came = swap(total[block:].astype(bf16), "ep", 2 * fast)
        earlier = came
        total = total[:block] + came.astype(f32)
        narrow = total.astype(bf16)
        attn.extend([total] + [swap(narrow, "ep", k).astype(f32) for k in range(1, fast)])
    attn = absolute(attn, upper * fast + near)
    hidden_state = jnp.concatenate(near_residual).astype(f32) + jnp.concatenate(attn, axis=1)

    scale = lax.rsqrt(jnp.mean(hidden_state * hidden_state, axis=-1, keepdims=True) + 1e-06)
    moe_in = (hidden_state * scale * moe_gain).astype(bf16)
    logits = jnp.dot(moe_in, router, preferred_element_type=f32)
    expert_count = router.shape[1]
    capacity = max(2, 3 * token_count // expert_count)
    expert_ids = jnp.stack(near_routes)
    route_hot = expert_ids[..., None] == jnp.arange(expert_count, dtype=jnp.int32)
    picked = jnp.sum(
        jnp.where(route_hot, logits.reshape(fast, token_count, 1, expert_count), 0.0), axis=-1
    )
    weights = jax.nn.sigmoid(picked - picked[..., ::-1])
    hot_flat = route_hot.reshape(fast, 2 * token_count, expert_count).astype(jnp.int32)
    earlier = jnp.cumsum(hot_flat, axis=1) - hot_flat
    slots = jnp.sum(earlier * hot_flat, axis=-1).reshape(fast, token_count, 2)
    group = fast * capacity
    source = jnp.arange(fast, dtype=jnp.int32)[:, None, None]
    target = ((expert_ids // fast) ^ far) * group + source * capacity + slots
    target = jnp.where(expert_ids % fast == near, target, -1).reshape(block, 2)
    hit = target[..., None] == jnp.arange(outer * group, dtype=jnp.int32)
    placement = jnp.any(hit, axis=1).astype(bf16)
    mixing = jnp.sum(jnp.where(hit, weights.reshape(block, 2, 1), 0.0), axis=1)

    outgoing = jnp.dot(placement.T, moe_in, preferred_element_type=f32).astype(bf16)
    arrived = [outgoing[k * group : (k + 1) * group] for k in range(outer)]
    for k in (2, 1):
        arrived[k] = swap(arrived[k], "ep", k * fast)
    arrived[3], _ = lax.optimization_barrier((arrived[3], arrived[1]))
    arrived[3] = swap(arrived[3], "ep", 3 * fast)
    blocks = n_ctx // 2
    over = [[swap(rows, "ctx", 2 * b) for b in range(1, blocks)] for rows in arrived]

    def visit(members, sooner, latest):
        chip = [arrived[k] for k in members]
        chip += [over[k][b] for b in range(blocks - 1) for k in members]
        chip, _ = lax.optimization_barrier((chip, sooner))
        chip = jnp.concatenate(chip)
        rows = jnp.concatenate([chip, swap(chip, "ctx", 1)])
        rows, _ = lax.optimization_barrier((rows, latest))
        partial = experts(rows, gate_weight[0], up_weight[0], down_weight[0])
        half = chip.shape[0]
        return partial[:half].astype(f32) + swap(partial[half:], "ctx", 1).astype(f32), partial

    def collect(summed, first, last):
        size = summed.shape[0] // blocks
        result = summed[first:last]
        for b in range(1, blocks):
            other = summed[b * size + first : b * size + last].astype(bf16)
            result = result + swap(other, "ctx", 2 * b).astype(f32)
        return result.astype(bf16)

    early, partial = visit((0, 1), (), (arrived[2], arrived[3]))
    second = collect(early, group, 2 * group)
    summed, _ = visit((2, 3), partial, ())
    summed, second = lax.optimization_barrier((summed, second))
    third = collect(summed, group, 2 * group)
    summed, early, third = lax.optimization_barrier((summed, early, third))
    returned = [
        collect(early, 0, group),
        swap(second, "ep", fast),
        swap(collect(summed, 0, group), "ep", 2 * fast),
        swap(third, "ep", 3 * fast),
    ]

    def weighted(shares, rows):
        high = shares.astype(bf16)
        low = (shares - high.astype(f32)).astype(bf16)
        out = jnp.dot(jnp.concatenate([high, low]), rows, preferred_element_type=f32)
        return out[: shares.shape[0]] + out[shares.shape[0] :]

    cut = lambda k: mixing[:, k * group : (k + 1) * group]
    total = weighted(
        jnp.concatenate([cut(0), cut(1), cut(3)], axis=1),
        jnp.concatenate([returned[0], returned[1], returned[3]]),
    )
    mine = lambda a: lax.dynamic_index_in_dim(
        a.reshape((fast, token_count) + a.shape[1:]), near, 0, False
    )
    result = mine(hidden_state) + mine(total)
    shares, rows = [mine(cut(2))], [returned[2]]
    own_ids, own_slots, own_weights = mine(expert_ids.reshape(block, 2)), mine(slots.reshape(block, 2)), mine(weights.reshape(block, 2))
    for k in range(1, fast):
        other = lax.dynamic_index_in_dim(
            total.reshape(fast, token_count, model), near ^ k, 0, False
        )
        result = result + swap(other.astype(bf16), "ep", k).astype(f32)
        theirs = lax.dynamic_slice_in_dim(returned[2], (near ^ k) * capacity, capacity, 0)
        rows.append(swap(theirs, "ep", k))
        named = own_ids == (far ^ 2) * fast + (near ^ k)
        there = named[..., None] & (
            own_slots[..., None] == jnp.arange(capacity, dtype=jnp.int32)
        )
        shares.append(jnp.sum(jnp.where(there, own_weights[..., None], 0.0), axis=1))
    result = result + weighted(jnp.concatenate(shares, axis=1), jnp.concatenate(rows))
    return result.astype(bf16).reshape(residual.shape)


def solution(mesh):
    return jax.shard_map(
        shards,
        mesh=mesh,
        in_specs=(
            P("ctx", None, "ep"),
            P("ctx", None, "ep"),
            P("ctx", None, "ep"),
            P("ep", None, "ctx"),
            P("ep"),
            P("ep", "ctx"),
            P(("ctx", "ep"), None, None),
            P(),
            P(),
            P("ep", None, "ctx"),
            P("ep", None, "ctx"),
            P("ep", "ctx", None),
            P(("ctx", "ep"), None, None),
        ),
        out_specs=P(("ctx", "ep"), None, None),
        check_vma=False,
    )
```
